32 devices in a mesh: branch: 16 (over z, x, core), head: 2 (over y).
Axes of the slice: x: 2, y: 2, z: 4, core: 2. Of those that a mesh axis runs over, the one named last changes fastest.
Arguments:
- queries: bfloat16 [4096, 8192], P('branch', 'head'), may hold values from -8 to 8
- branch_keys: bfloat16 [4096, 1024], P('branch', 'head'), may hold values from -6 to 6
- branch_values: bfloat16 [4096, 1024], P('branch', 'head'), may hold values from -6 to 6
- prompt_keys: bfloat16 [768, 1024], P(('branch', 'head')), may hold values from -6 to 6
- prompt_values: bfloat16 [768, 1024], P(('branch', 'head')), may hold values from -6 to 6
- parent: int32 [16], replicated, may hold values from -1 to 15, as said below
- fork_tokens: int32 [16], replicated, may hold values from 0 to 256, as said below
- lengths: int32 [16], replicated, may hold values from 64 to 256
Outputs:
- attended: bfloat16 [4096, 8192], P('branch', 'head')
The draws below stay inside these ranges and needn't reach their ends.
Inputs may be any that keep to these rules, and one draw needn't show every extreme that they name: Exactly 2 branches have parent -1, and every other branch's parent is one of them. `fork_tokens`: 0 where parent is -1, else at most the parent's length.
All inputs are finite; a program needn't handle non-finite values.
Results may differ from the reference program's by a relative error of at most 0.0045.
Values may be sent and summed in bfloat16 or wider, within the bound.
A program may use at most 64 MiB of HBM per device.

```python
import math
import jax
import jax.numpy as jnp
from jax import lax

HEADS = 64
KV_HEADS = 8
HEAD_DIM = 128
TOK = 256
NB = 16
PROMPT = 768


def tree_draw(key):
    folded = jax.random.fold_in(key, 7)
    key_perm, key_len, key_limit, key_slot, key_fork = jax.random.split(folded, 5)
    order_table = jax.random.permutation(key_perm, NB).astype(jnp.int32)
    positions = jnp.arange(NB, dtype=jnp.int32)
    last_at = jnp.sum(jnp.where(order_table == NB - 1, positions, 0)).astype(jnp.int32)
    first_entry = order_table[0]
    order_table = order_table.at[last_at].set(first_entry).at[0].set(NB - 1).astype(jnp.int32)
    ranking = jnp.argsort(order_table, stable=True).astype(jnp.int32)
    root_count = NB // 8
    is_root = ranking < root_count
    lengths = jax.random.randint(key_len, (NB,), TOK // 4, TOK + 1).astype(jnp.int32)
    lengths = lengths.at[order_table[0]].set(TOK).at[order_table[1]].set(TOK // 4)
    slot_limit = jax.random.randint(key_limit, (NB,), 1, root_count + 1)
    slot_pick = jax.random.randint(key_slot, (NB,), 0, slot_limit)
    slot_pick = jnp.where(ranking == root_count, 0, slot_pick)
    parent = jnp.where(is_root, -1, order_table[slot_pick]).astype(jnp.int32)
    parent_safe = jnp.maximum(parent, 0)
    fork_tokens = jax.random.randint(key_fork, (NB,), 1, lengths[parent_safe] + 1)
    fork_tokens = jnp.where(ranking == root_count, TOK, fork_tokens)
    fork_tokens = jnp.where(is_root, 0, fork_tokens).astype(jnp.int32)
    return (parent, fork_tokens, lengths, ranking)


def draw_parent(key, part):
    return tree_draw(key)[0]


def draw_fork_tokens(key, part):
    return tree_draw(key)[1]


def draw_lengths(key, part):
    return tree_draw(key)[2]


def query_damping(key):
    ranking = tree_draw(key)[3]
    root_count = NB // 8
    damped = (ranking % 4 == 0) | (ranking == root_count)
    row_branch = jnp.arange(NB * TOK, dtype=jnp.int32) // TOK
    return jnp.where(damped[row_branch], 0.25, 1.0).astype(jnp.float32)


def draw_queries(key, part):
    folded = jax.random.fold_in(key, 13)
    shape_full = (NB * TOK, HEADS * HEAD_DIM)
    damping = query_damping(key)
    drawn = jnp.clip(2.5 * jax.random.normal(folded, shape_full, jnp.float32), -8.0, 8.0)
    drawn = drawn * damping[:, None]
    return drawn.astype(jnp.bfloat16)


def draw_prompt_keys(key, part):
    folded = jax.random.fold_in(key, 17)
    shape_full = (PROMPT, KV_HEADS * HEAD_DIM)
    drawn = jnp.clip(jax.random.normal(folded, shape_full, jnp.float32), -6.0, 6.0)
    return drawn.astype(jnp.bfloat16)


def level_of(stream_key, shape, cuts, low, largest):
    def one(dim, blocks):
        heights = jax.random.uniform(jax.random.fold_in(jax.random.fold_in(stream_key, 6), dim), (blocks,), jnp.float32, low / len(cuts), largest / len(cuts))
        return jnp.repeat(jnp.exp(heights), shape[dim] // blocks).reshape((-1,) + (1,) * (len(shape) - dim - 1))

    factor_of = one(*cuts[0])
    for cut in cuts[1:]:
        factor_of = factor_of * one(*cut)
    return factor_of


def centred(own_key, extent, spread, bound, cuts=(), kind=jnp.bfloat16):
    level = level_of(own_key, extent, cuts, -0.22, 0.18) if cuts else 1.0
    entries = jax.random.normal(own_key, extent, jnp.float32) * spread * level
    return jnp.minimum(jnp.maximum(entries, -bound), bound).astype(kind)


def setup_inputs(seed: int = 0) -> dict:
    key_of = jax.random.split(jax.random.key(seed), 9)
    queries = draw_queries(jax.random.fold_in(key_of[8], 71), 0)
    branch_keys = centred(key_of[1], (NB * TOK, KV_HEADS * HEAD_DIM), 1.0, 6.0, ((0, 16), (1, 2)))
    branch_values = centred(key_of[2], (NB * TOK, KV_HEADS * HEAD_DIM), 1.0, 6.0, ((0, 16), (1, 2)))
    prompt_keys = draw_prompt_keys(jax.random.fold_in(key_of[8], 71), 0)
    prompt_values = centred(key_of[4], (PROMPT, KV_HEADS * HEAD_DIM), 1.0, 6.0, ((0, 32),))
    parent = draw_parent(jax.random.fold_in(key_of[8], 71), 0)
    fork_tokens = draw_fork_tokens(jax.random.fold_in(key_of[8], 71), 0)
    lengths = draw_lengths(jax.random.fold_in(key_of[8], 71), 0)
    return dict(queries=queries, branch_keys=branch_keys, branch_values=branch_values, prompt_keys=prompt_keys, prompt_values=prompt_values, parent=parent, fork_tokens=fork_tokens, lengths=lengths)


def reference(queries, branch_keys, branch_values, prompt_keys, prompt_values, parent, fork_tokens, lengths):
    branches = parent.shape[0]
    tok_rows = queries.shape[0] // branches
    groups = KV_HEADS
    per_group = HEADS // KV_HEADS
    score_scale = 1.0 / math.sqrt(HEAD_DIM)
    prompt_len = prompt_keys.shape[0]
    prompt_key_f = prompt_keys.astype(jnp.float32).reshape(prompt_len, groups, HEAD_DIM)
    prompt_value_f = prompt_values.astype(jnp.float32).reshape(prompt_len, groups, HEAD_DIM)
    query_pos = jnp.arange(tok_rows, dtype=jnp.int32)

    def take_rows(source, first):
        return lax.dynamic_slice_in_dim(source, first, tok_rows, 0).astype(jnp.float32).reshape(tok_rows, groups, HEAD_DIM)

    def per_branch(branch):
        row_start = (branch * tok_rows).astype(jnp.int32)
        parent_id = parent[branch]
        parent_start = (jnp.maximum(parent_id, 0) * tok_rows).astype(jnp.int32)
        query_f = lax.dynamic_slice_in_dim(queries, row_start, tok_rows, 0).astype(jnp.float32)
        query_f = query_f.reshape(tok_rows, groups, per_group, HEAD_DIM)
        key_all = jnp.concatenate([prompt_key_f, take_rows(branch_keys, parent_start), take_rows(branch_keys, row_start)], 0)
        value_all = jnp.concatenate([prompt_value_f, take_rows(branch_values, parent_start), take_rows(branch_values, row_start)], 0)
        from_parent = (parent_id >= 0) & (query_pos < fork_tokens[branch])
        visible = jnp.concatenate([jnp.ones((tok_rows, prompt_len), dtype=bool), jnp.broadcast_to(from_parent[None, :], (tok_rows, tok_rows)), query_pos[None, :] <= query_pos[:, None]], 1)
        scores = jnp.einsum('tgqd,ngd->tgqn', query_f, key_all) * score_scale
        scores = jnp.where(visible[:, None, None, :], scores, -jnp.inf)
        row_max = lax.optimization_barrier(jnp.max(scores, axis=-1, keepdims=True))
        weights = jnp.exp(scores - row_max)
        denominator = lax.optimization_barrier(jnp.sum(weights, axis=-1))
        weights_low = lax.optimization_barrier(weights.astype(jnp.bfloat16)).astype(jnp.float32)
        numerator = jnp.einsum('tgqn,ngd->tgqd', weights_low, value_all)
        output = numerator / denominator[..., None]
        live = query_pos < lengths[branch]
        output = jnp.where(live[:, None, None, None], output, 0.0)
        return output.reshape(tok_rows, HEADS * HEAD_DIM).astype(jnp.bfloat16)
    results = lax.map(per_branch, jnp.arange(branches, dtype=jnp.int32))
    return results.reshape(branches * tok_rows, HEADS * HEAD_DIM)
```

```python
import functools
import math

import jax
import jax.numpy as jnp
from jax import lax
from jax.experimental import pallas as pl
from jax.experimental.pallas import tpu as pltpu
from jax.sharding import PartitionSpec as P

HEADS = 64
KV_HEADS = 8
HEAD_DIM = 128
MESH = pl.DeviceIdType.MESH
F32 = jnp.float32
BF16 = jnp.bfloat16


def place(n):
    me = lax.axis_index("branch")
    return me, me // 4, (me // 2) % 2, me % 2, lax.axis_index("head")


def root_rank(parent_ref, index, n):
    before = jnp.int32(0)
    for j in range(n):
        is_root = jnp.where(parent_ref[j] < 0, 1, 0)
        before = before + jnp.where(j < index, is_root, 0)
    return parent_ref[index] < 0, before


def comm_kernel(
    n, heads_n, roots, parent_ref, bk_ref, bv_ref, pk_ref, pv_ref, prompt_out, roots_out,
    sib_kv, cand, x_in, part, z_in, y_out, y_in, send_sem, recv_sem,
):
    Z = n // 4
    half = bk_ref.shape[0] // 2
    cols = bk_ref.shape[1]
    rz = 2 * half // Z
    me, z, x, c, h = place(n)
    sib = me + 1 - 2 * c
    xp = me + 2 - 4 * x

    def zpeer(d):
        return lax.rem(z + d, Z) * 4 + x * 2 + c

    def zfrom(d):
        return lax.rem(z + Z - d, Z)

    counter = [0]
    copies = []

    def copy(src, dst, b, hh=None):
        k = counter[0]
        counter[0] += 1
        cp = pltpu.make_async_remote_copy(
            src_ref=src, dst_ref=dst, send_sem=send_sem.at[k], recv_sem=recv_sem.at[k],
            device_id=(b, h if hh is None else hh), device_id_type=MESH,
        )
        cp.start()
        copies.append(cp)
        return cp

    barrier = pltpu.get_barrier_semaphore()
    peers = [(sib, h), (xp, h)] + [(zpeer(d), h) for d in range(1, Z)]
    if heads_n == 2:
        peers.append((me, 1 - h))
    for peer in peers:
        pl.semaphore_signal(barrier, inc=1, device_id=peer, device_id_type=MESH)
    pl.semaphore_wait(barrier, len(peers))

    theirs = pl.ds(pl.multiple_of((1 - c) * half, half), half)
    mine = pl.ds(pl.multiple_of(c * half, half), half)
    cp_k = copy(bk_ref.at[theirs], sib_kv.at[0], sib)
    cp_v = copy(bv_ref.at[theirs], sib_kv.at[1], sib)

    if heads_n == 2:
        rows = pk_ref.shape[0]
        away = pl.ds(pl.multiple_of((1 - h) * cols, cols), cols)
        home = pl.ds(pl.multiple_of(h * cols, cols), cols)
        pad = jnp.zeros((y_out.shape[1] - rows, cols), F32)
        for i, ref in enumerate((pk_ref, pv_ref)):
            y_out[i] = jnp.concatenate([ref[:, away].astype(F32), pad], 0).astype(BF16)
        cp_y = copy(y_out, y_in, me, 1 - h)

    is_me, rank_me = root_rank(parent_ref, me, n)
    is_sib, rank_sib = root_rank(parent_ref, sib, n)
    cp_k.wait_recv()
    cp_v.wait_recv()
    for r in range(roots):
        w_me = jnp.where(is_me & (rank_me == r), 1.0, 0.0).astype(F32)
        w_sib = jnp.where(is_sib & (rank_sib == r), 1.0, 0.0).astype(F32)
        for i, ref in enumerate((bk_ref, bv_ref)):
            total = ref[mine, :].astype(F32) * w_me + sib_kv[i].astype(F32) * w_sib
            cand[r // 2, r % 2, i * half : (i + 1) * half] = total.astype(BF16)
    cp_x = copy(cand.at[:, 1 - x], x_in, xp)

    if heads_n == 2:
        cp_y.wait_recv()
        for i, ref in enumerate((pk_ref, pv_ref)):
            prompt_out[me, i] = jnp.concatenate(
                [ref[:, home].astype(F32), y_in[i, :rows].astype(F32)], 0
            ).astype(BF16)
    else:
        prompt_out[me, 0] = pk_ref[...]
        prompt_out[me, 1] = pv_ref[...]
    slab = prompt_out.at[me]
    cp_pz = {d: copy(slab, slab, zpeer(d)) for d in range(1, Z)}
    cp_px = {0: copy(slab, slab, xp)}
    cp_ps = [copy(slab, slab, sib)]

    cp_x.wait_recv()
    for j in range(roots // 2):
        part[j] = (cand[j, x].astype(F32) + x_in[j].astype(F32)).astype(BF16)

    def zrows(zz):
        return pl.ds(pl.multiple_of(zz * rz, rz), rz)

    cp_rs = {
        d: copy(part.at[:, zrows(lax.rem(z + d, Z))], z_in.at[d - 1], zpeer(d))
        for d in range(1, Z)
    }

    for d in range(1, Z):
        cp_pz[d].wait_recv()
        got = prompt_out.at[zfrom(d) * 4 + x * 2 + c]
        cp_px[d] = copy(got, got, xp)
        cp_ps.append(copy(got, got, sib))

    for d in range(1, Z):
        cp_rs[d].wait_recv()
    for j in range(roots // 2):
        total = part[j, zrows(z)].astype(F32)
        for d in range(1, Z):
            total = total + z_in[d - 1, j].astype(F32)
        roots_out[c, j, x, zrows(z)] = total.astype(BF16)

    def piece(xx, zz):
        return roots_out.at[c, :, xx, zrows(zz)]

    cp_gz = {d: copy(piece(x, z), piece(x, z), zpeer(d)) for d in range(1, Z)}
    cp_gx = {0: copy(piece(x, z), piece(x, z), xp)}
    cp_gs = [copy(piece(x, z), piece(x, z), sib)]

    for d in range(0, Z):
        cp_px[d].wait_recv()
        got = prompt_out.at[zfrom(d) * 4 + (1 - x) * 2 + c]
        cp_ps.append(copy(got, got, sib))

    for d in range(1, Z):
        cp_gz[d].wait_recv()
        got = piece(x, zfrom(d))
        cp_gx[d] = copy(got, got, xp)
        cp_gs.append(copy(got, got, sib))
    for d in range(0, Z):
        cp_gx[d].wait_recv()
        got = piece(1 - x, zfrom(d))
        cp_gs.append(copy(got, got, sib))
    for cp in cp_ps + cp_gs:
        cp.wait_recv()
    for cp in copies:
        cp.wait_send()


def attend_kernel(
    n, roots, parent_ref, fork_ref, length_ref, q_ref, bk_ref, bv_ref, prompt_ref, roots_ref,
    out_ref, keys, values,
):
    tok = q_ref.shape[0]
    half = tok // 2
    per_group = q_ref.shape[1] // HEAD_DIM
    prompt_rows = prompt_ref.shape[0] * prompt_ref.shape[2]
    scale = math.log2(math.e) / math.sqrt(HEAD_DIM)
    me = lax.axis_index("branch")
    up = jnp.maximum(parent_ref[me], 0)
    _, slot = root_rank(parent_ref, up, n)
    slot = jnp.minimum(slot, roots - 1)
    fork = fork_ref[me]

    own = prompt_rows + tok
    keys[:prompt_rows] = prompt_ref[:, 0].reshape(prompt_rows, HEAD_DIM)
    values[:prompt_rows, :HEAD_DIM] = prompt_ref[:, 1].reshape(prompt_rows, HEAD_DIM)
    values[:prompt_rows, HEAD_DIM:] = jnp.ones((prompt_rows, HEAD_DIM), BF16)
    keys[own:] = bk_ref[...]
    values[own:, :HEAD_DIM] = bv_ref[...]
    values[own:, HEAD_DIM:] = jnp.ones((tok, HEAD_DIM), BF16)
    first = bk_ref[0:1, :].astype(F32)
    for i in range(2):
        rows = slice(prompt_rows + i * half, prompt_rows + (i + 1) * half)
        seen = i * half + lax.broadcasted_iota(jnp.int32, (half, HEAD_DIM), 0) < fork
        parent_k = roots_ref[i, slot // 2, slot % 2, :half].astype(F32)
        parent_v = roots_ref[i, slot // 2, slot % 2, half:].astype(F32)
        keys[rows] = jnp.where(seen, parent_k, first).astype(BF16)
        values[rows, :HEAD_DIM] = jnp.where(seen, parent_v, 0.0).astype(BF16)
        values[rows, HEAD_DIM:] = jnp.where(seen, 1.0, 0.0).astype(BF16)

    row = lax.broadcasted_iota(jnp.int32, (tok, tok), 0)
    causal = lax.broadcasted_iota(jnp.int32, (tok, tok), 1) <= row
    live = lax.broadcasted_iota(jnp.int32, (tok, HEAD_DIM), 0) < length_ref[me]
    for head in range(per_group):
        cols = slice(head * HEAD_DIM, (head + 1) * HEAD_DIM)
        q = q_ref[:, cols]
        contract = (((1,), (1,)), ((), ()))
        s_far = lax.dot_general(q, keys[:own], contract, preferred_element_type=F32)
        s_own = lax.dot_general(q, keys[own:], contract, preferred_element_type=F32)
        s_own = jnp.where(causal, s_own, -1e30)
        top = jnp.maximum(
            jnp.max(s_far, axis=1, keepdims=True), jnp.max(s_own, axis=1, keepdims=True)
        )
        p_far = jnp.exp2((s_far - top) * scale).astype(BF16)
        p_own = jnp.exp2((s_own - top) * scale).astype(BF16)
        total = jnp.dot(p_far, values[:own], preferred_element_type=F32) + jnp.dot(
            p_own, values[own:], preferred_element_type=F32
        )
        result = total[:, :HEAD_DIM] / total[:, HEAD_DIM:]
        out_ref[:, cols] = jnp.where(live, result, 0.0).astype(BF16)


def body(
    n, heads_n, queries, branch_keys, branch_values, prompt_keys, prompt_values, parent,
    fork_tokens, lengths,
):
    tok, cols = branch_keys.shape
    groups = cols // HEAD_DIM
    per_group = HEADS // KV_HEADS
    roots = n // 8
    Z = n // 4
    half = tok // 2
    rz = tok // Z
    rows = prompt_keys.shape[0]
    slab_rows = rows * heads_n
    if heads_n != 2:
        prompt_keys = lax.all_to_all(prompt_keys, "head", split_axis=1, concat_axis=0, tiled=True)
        prompt_values = lax.all_to_all(
            prompt_values, "head", split_axis=1, concat_axis=0, tiled=True
        )
    padded = -(-rows // 16) * 16
    vmem = pl.BlockSpec(memory_space=pltpu.VMEM)
    smem = pl.BlockSpec(memory_space=pltpu.SMEM)
    n_copies = 32 + 10 * Z
    prompt_all, roots_all = pl.pallas_call(
        functools.partial(comm_kernel, n, heads_n, roots),
        out_shape=(
            jax.ShapeDtypeStruct((n, 2, slab_rows, cols), BF16),
            jax.ShapeDtypeStruct((2, roots // 2, 2, tok, cols), BF16),
        ),
        in_specs=[smem] + [vmem] * 4,
        out_specs=(vmem, vmem),
        scratch_shapes=[
            pltpu.VMEM((2, half, cols), BF16),
            pltpu.VMEM((roots // 2, 2, tok, cols), BF16),
            pltpu.VMEM((roots // 2, tok, cols), BF16),
            pltpu.VMEM((roots // 2, tok, cols), BF16),
            pltpu.VMEM((Z - 1, roots // 2, rz, cols), BF16),
            pltpu.VMEM((2, padded, cols), BF16),
            pltpu.VMEM((2, padded, cols), BF16),
            pltpu.SemaphoreType.DMA((n_copies,)),
            pltpu.SemaphoreType.DMA((n_copies,)),
        ],
        compiler_params=pltpu.CompilerParams(
            collective_id=0, has_side_effects=True, vmem_limit_bytes=48 * 2**20
        ),
    )(parent, branch_keys, branch_values, prompt_keys, prompt_values)

    wide = per_group * HEAD_DIM
    total_rows = n * slab_rows + 2 * tok
    return pl.pallas_call(
        functools.partial(attend_kernel, n, roots),
        out_shape=jax.ShapeDtypeStruct(queries.shape, BF16),
        grid=(groups,),
        in_specs=[
            smem, smem, smem,
            pl.BlockSpec((tok, wide), lambda g: (0, g)),
            pl.BlockSpec((tok, HEAD_DIM), lambda g: (0, g)),
            pl.BlockSpec((tok, HEAD_DIM), lambda g: (0, g)),
            pl.BlockSpec((n, 2, slab_rows, HEAD_DIM), lambda g: (0, 0, 0, g)),
            pl.BlockSpec((2, roots // 2, 2, tok, HEAD_DIM), lambda g: (0, 0, 0, 0, g)),
        ],
        out_specs=pl.BlockSpec((tok, wide), lambda g: (0, g)),
        scratch_shapes=[
            pltpu.VMEM((total_rows, HEAD_DIM), BF16),
            pltpu.VMEM((total_rows, 2 * HEAD_DIM), BF16),
        ],
        compiler_params=pltpu.CompilerParams(vmem_limit_bytes=48 * 2**20),
    )(parent, fork_tokens, lengths, queries, branch_keys, branch_values, prompt_all, roots_all)


def solution(mesh):
    placed = (
        P("branch", "head"),
        P("branch", "head"),
        P("branch", "head"),
        P(("branch", "head"), None),
        P(("branch", "head"), None),
        P(),
        P(),
        P(),
    )
    return jax.shard_map(
        functools.partial(body, mesh.shape["branch"], mesh.shape["head"]),
        mesh=mesh, in_specs=placed, out_specs=P("branch", "head"), check_vma=False,
    )
```

```python
import functools
import math

import jax
import jax.numpy as jnp
from jax import lax
from jax.experimental import pallas as pl
from jax.experimental.pallas import tpu as pltpu
from jax.sharding import PartitionSpec as P

HEADS = 64
KV_HEADS = 8
HEAD_DIM = 128
MESH = pl.DeviceIdType.MESH
F32 = jnp.float32
BF16 = jnp.bfloat16


def place(n):
    me = lax.axis_index("branch")
    return me, me // 4, (me // 2) % 2, me % 2, lax.axis_index("head")


def root_rank(parent_ref, index, n):
    before = jnp.int32(0)
    for j in range(n):
        before = before + jnp.where((parent_ref[j] < 0) & (j < index), 1, 0)
    return before


def tree_kernel(
    n, heads_n, roots, chunks,
    parent_hbm, fork_hbm, length_hbm, q_hbm, bk_hbm, bv_hbm, pk_hbm, pv_hbm,
    out_hbm,
    q_ref, out_ref, keys_out, values_out, live_out, parent_ref, fork_ref, length_ref, bk_ref, bv_ref, pk_ref, pv_ref, roots_all,
    prompt_out, acc, tops, sib_kv, cand, x_in, part, z_in, y_out, y_in,
    send_sem, recv_sem, local_sem, out_sem,
):
    Z = n // 4
    tok, cols = bk_ref.shape
    half = tok // 2
    crows = tok // chunks
    rz = crows // Z
    groups = cols // HEAD_DIM
    per_group = q_ref.shape[1] // cols
    run = per_group // 2
    blocks = 2 * groups
    scale = math.log2(math.e) / math.sqrt(HEAD_DIM)
    contract = (((1,), (1,)), ((), ()))
    me, z, x, c, h = place(n)
    sib = me + 1 - 2 * c
    xp = me + 2 - 4 * x

    def zpeer(d):
        return lax.rem(z + d, Z) * 4 + x * 2 + c

    def zfrom(d):
        return lax.rem(z + Z - d, Z)

    local = []
    for i, (src, dst) in enumerate((
        (pk_hbm, pk_ref), (pv_hbm, pv_ref), (bk_hbm, bk_ref), (bv_hbm, bv_ref),
        (parent_hbm, parent_ref), (fork_hbm, fork_ref), (length_hbm, length_ref), (q_hbm, q_ref),
    )):
        cp = pltpu.make_async_copy(src, dst, local_sem.at[i])
        cp.start()
        local.append(cp)

    counter = [0]
    copies = []

    def copy(src, dst, b, hh=None):
        k = counter[0]
        counter[0] += 1
        cp = pltpu.make_async_remote_copy(
            src_ref=src, dst_ref=dst, send_sem=send_sem.at[k], recv_sem=recv_sem.at[k],
            device_id=(b, h if hh is None else hh), device_id_type=MESH,
        )
        cp.start()
        copies.append(cp)
        return cp

    def own_part(block):
        g = block // 2
        lanes = pl.ds(pl.multiple_of(g * HEAD_DIM, HEAD_DIM), HEAD_DIM)
        row = lax.broadcasted_iota(jnp.int32, (tok, tok), 0)
        causal = lax.broadcasted_iota(jnp.int32, (tok, tok), 1) <= row
        k = bk_ref[:, lanes]
        v = jnp.concatenate([bv_ref[:, lanes], jnp.ones((tok, HEAD_DIM), BF16)], 1)
        for i in range(run):
            head = block * run + i
            q = q_ref[:, pl.ds(pl.multiple_of(head * HEAD_DIM, HEAD_DIM), HEAD_DIM)]
            s = lax.dot_general(q, k, contract, preferred_element_type=F32)
            s = jnp.where(causal, s, -1e30)
            top = jnp.max(s, axis=1, keepdims=True)
            p = jnp.exp2((s - top) * scale).astype(BF16)
            acc[head] = jnp.dot(p, v, preferred_element_type=F32)
            tops[head] = jnp.broadcast_to(top, (tok, HEAD_DIM))

    def prompt_part(block):
        g = block // 2
        lanes = slice(g * HEAD_DIM, (g + 1) * HEAD_DIM)
        k = prompt_out[:, 0, :, lanes].reshape(-1, HEAD_DIM)
        v = prompt_out[:, 1, :, lanes].reshape(-1, HEAD_DIM)
        v = jnp.concatenate([v, jnp.ones(v.shape, BF16)], 1)
        for i in range(run):
            head = block * run + i
            q = q_ref[:, head * HEAD_DIM : (head + 1) * HEAD_DIM]
            total, top = absorb(head, q, k, v)
            acc[head] = total
            tops[head] = top

    def absorb(head, q, k, v):
        s = lax.dot_general(q, k, contract, preferred_element_type=F32)
        before = tops[head]
        top = jnp.maximum(before, jnp.max(s, axis=1, keepdims=True))
        p = jnp.exp2((s - top[:, :1]) * scale).astype(BF16)
        fade = jnp.exp2((before - top) * scale)
        fade = jnp.concatenate([fade, fade], 1)
        return jnp.dot(p, v, preferred_element_type=F32) + acc[head] * fade, top

    wide = per_group * HEAD_DIM

    def out_copy(g):
        span = pl.ds(pl.multiple_of(g * wide, wide), wide)
        return pltpu.make_async_copy(out_ref.at[:, span], out_hbm.at[:, span], out_sem.at[g])

    def parent_part(g, carry):
        k = keys_out[:, pl.ds(pl.multiple_of(g * HEAD_DIM, HEAD_DIM), HEAD_DIM)]
        v = values_out[:, pl.ds(pl.multiple_of(g * 2 * HEAD_DIM, 2 * HEAD_DIM), 2 * HEAD_DIM)]
        live = live_out[...] > 0.5
        for i in range(per_group):
            head = g * per_group + i
            here = pl.ds(pl.multiple_of(head * HEAD_DIM, HEAD_DIM), HEAD_DIM)
            total, _ = absorb(head, q_ref[:, here], k, v)
            result = total[:, :HEAD_DIM] / total[:, HEAD_DIM:]
            out_ref[:, here] = jnp.where(live, result, 0.0).astype(BF16)
        out_copy(g).start()
        return carry

    barrier = pltpu.get_barrier_semaphore()
    peers = [(sib, h), (xp, h)] + [(zpeer(d), h) for d in range(1, Z)]
    if heads_n == 2:
        peers.append((me, 1 - h))
    for peer in peers:
        pl.semaphore_signal(barrier, inc=1, device_id=peer, device_id_type=MESH)
    pl.semaphore_wait(barrier, len(peers))

    theirs = pl.ds(pl.multiple_of((1 - c) * half, half), half)
    mine = pl.ds(pl.multiple_of(c * half, half), half)
    cp_kv = [copy(bk_hbm.at[theirs], sib_kv.at[0], sib), copy(bv_hbm.at[theirs], sib_kv.at[1], sib)]

    local[0].wait()
    local[1].wait()
    if heads_n == 2:
        rows = pk_ref.shape[0]
        away = pl.ds(pl.multiple_of((1 - h) * cols, cols), cols)
        home = pl.ds(pl.multiple_of(h * cols, cols), cols)
        pad = jnp.zeros((y_out.shape[1] - rows, cols), F32)
        for i, ref in enumerate((pk_ref, pv_ref)):
            y_out[i] = jnp.concatenate([ref[:, away].astype(F32), pad], 0).astype(BF16)
        cp_y = copy(y_out, y_in, me, 1 - h)

    for cp in local[2:]:
        cp.wait()
    is_me, rank_me = parent_ref[me] < 0, root_rank(parent_ref, me, n)
    is_sib, rank_sib = parent_ref[sib] < 0, root_rank(parent_ref, sib, n)

    cp_x = []
    for i, ref in enumerate((bk_ref, bv_ref)):
        cp_kv[i].wait_recv()
        for r in range(roots):
            w_me = jnp.where(is_me & (rank_me == r), 1.0, 0.0).astype(F32)
            w_sib = jnp.where(is_sib & (rank_sib == r), 1.0, 0.0).astype(F32)
            total = ref[mine, :].astype(F32) * w_me + sib_kv[i].astype(F32) * w_sib
            cand[r // 2, r % 2, i * half : (i + 1) * half] = total.astype(BF16)
        if chunks == 2 or i == 1:
            span = slice((i + 1) * half - crows, (i + 1) * half)
            cp_x.append(copy(cand.at[:, 1 - x, span], x_in.at[:, span], xp))

    if heads_n == 2:
        cp_y.wait_recv()
        for i, ref in enumerate((pk_ref, pv_ref)):
            prompt_out[me, i] = jnp.concatenate(
                [ref[:, home].astype(F32), y_in[i, :rows].astype(F32)], 0
            ).astype(BF16)
    else:
        prompt_out[me, 0] = pk_ref[...]
        prompt_out[me, 1] = pv_ref[...]
    slab = prompt_out.at[me]
    cp_pz = {d: copy(slab, slab, zpeer(d)) for d in range(1, Z)}
    cp_px = {0: copy(slab, slab, xp)}
    cp_ps = [copy(slab, slab, sib)]

    def own_loop(block, carry):
        own_part(block)
        return carry

    lax.fori_loop(0, blocks, own_loop, 0)

    def zrows(ch, zz):
        return pl.ds(pl.multiple_of(ch * crows + zz * rz, rz), rz)

    cp_rs = {}
    for ch in range(chunks):
        cp_x[ch].wait_recv()
        span = slice(ch * crows, (ch + 1) * crows)
        for j in range(roots // 2):
            part[j, span] = (cand[j, x, span].astype(F32) + x_in[j, span].astype(F32)).astype(BF16)
        for d in range(1, Z):
            cp_rs[ch, d] = copy(
                part.at[:, zrows(ch, lax.rem(z + d, Z))], z_in.at[ch, d - 1], zpeer(d)
            )

    def piece(ch, xx, zz):
        return roots_all.at[c, :, xx, zrows(ch, zz)]

    cp_gz, cp_gx, cp_gs = {}, {}, []

    def reduce_step(ch):
        for d in range(1, Z):
            cp_rs[ch, d].wait_recv()
        for j in range(roots // 2):
            total = part[j, zrows(ch, z)].astype(F32)
            for d in range(1, Z):
                total = total + z_in[ch, d - 1, j].astype(F32)
            roots_all[c, j, x, zrows(ch, z)] = total.astype(BF16)
        own = piece(ch, x, z)
        for d in range(1, Z):
            cp_gz[ch, d] = copy(own, own, zpeer(d))
        cp_gx[ch, 0] = copy(own, own, xp)
        cp_gs.append(copy(own, own, sib))

    def gather_step(ch):
        for d in range(1, Z):
            cp_gz[ch, d].wait_recv()
            got = piece(ch, x, zfrom(d))
            cp_gx[ch, d] = copy(got, got, xp)
            cp_gs.append(copy(got, got, sib))

    def last_step(ch):
        for d in range(0, Z):
            cp_gx[ch, d].wait_recv()
            got = piece(ch, 1 - x, zfrom(d))
            cp_gs.append(copy(got, got, sib))

    for d in range(1, Z):
        cp_pz[d].wait_recv()
        got = prompt_out.at[zfrom(d) * 4 + x * 2 + c]
        cp_px[d] = copy(got, got, xp)
        cp_ps.append(copy(got, got, sib))
    reduce_step(0)
    for d in range(0, Z):
        cp_px[d].wait_recv()
        got = prompt_out.at[zfrom(d) * 4 + (1 - x) * 2 + c]
        cp_ps.append(copy(got, got, sib))
    if chunks == 2:
        reduce_step(1)
    for cp in cp_ps:
        cp.wait_recv()

    at = {}
    for step, ch, when in (
        (gather_step, 0, 3), (gather_step, 1, 6), (last_step, 0, 7), (last_step, 1, 8)
    ):
        if ch < chunks:
            at.setdefault(max(when * blocks // 8 - 1, 0), []).append((step, ch))
    for block in range(blocks):
        prompt_part(block)
        for step, ch in at.get(block, []):
            step(ch)

    rank = root_rank(parent_ref, jnp.maximum(parent_ref[me], 0), n)
    fork = fork_ref[me]
    weights = [jnp.where(rank == r, 1.0, 0.0).astype(F32) for r in range(roots)]
    live_out[...] = jnp.where(
        lax.broadcasted_iota(jnp.int32, (tok, HEAD_DIM), 0) < length_ref[me], 1.0, 0.0
    )
    for cp in cp_gs:
        cp.wait_recv()
    first = bk_ref[0:1, :].astype(F32)
    for i in range(2):
        out_rows = slice(i * half, (i + 1) * half)
        seen = i * half + lax.broadcasted_iota(jnp.int32, (half, cols), 0) < fork
        sums = []
        for start in (0, half):
            total = jnp.zeros((half, cols), F32)
            for r in range(roots):
                total = total + weights[r] * roots_all[
                    i, r // 2, r % 2, start : start + half
                ].astype(F32)
            sums.append(total)
        keys_out[out_rows] = jnp.where(seen, sums[0], first).astype(BF16)
        values = jnp.where(seen, sums[1], 0.0).astype(BF16)
        ones = jnp.where(seen[:, :HEAD_DIM], 1.0, 0.0).astype(BF16)
        for g in range(groups):
            values_out[out_rows, 2 * g * HEAD_DIM : (2 * g + 1) * HEAD_DIM] = values[
                :, g * HEAD_DIM : (g + 1) * HEAD_DIM
            ]
            values_out[out_rows, (2 * g + 1) * HEAD_DIM : (2 * g + 2) * HEAD_DIM] = ones
    lax.fori_loop(0, groups, parent_part, 0)
    for cp in copies:
        cp.wait_send()
    for g in range(groups):
        out_copy(g).wait()


def body(
    n, heads_n, queries, branch_keys, branch_values, prompt_keys, prompt_values, parent,
    fork_tokens, lengths,
):
    tok, cols = branch_keys.shape
    groups = cols // HEAD_DIM
    per_group = HEADS // KV_HEADS
    roots = n // 8
    Z = n // 4
    half = tok // 2
    rows = prompt_keys.shape[0]
    slab_rows = rows * heads_n
    if heads_n != 2:
        prompt_keys = lax.all_to_all(prompt_keys, "head", split_axis=1, concat_axis=0, tiled=True)
        prompt_values = lax.all_to_all(
            prompt_values, "head", split_axis=1, concat_axis=0, tiled=True
        )
    padded = -(-rows // 16) * 16
    hbm = pl.BlockSpec(memory_space=pltpu.HBM)
    chunks = 2 if half % (16 * Z) == 0 else 1
    rz = tok // chunks // Z
    n_copies = 16 + 16 * Z
    width = queries.shape[1]
    heads = width // HEAD_DIM
    return pl.pallas_call(
        functools.partial(tree_kernel, n, heads_n, roots, chunks),
        out_shape=jax.ShapeDtypeStruct((tok, width), BF16),
        in_specs=[hbm] * 8,
        out_specs=hbm,
        scratch_shapes=[
            pltpu.VMEM((tok, width), BF16),
            pltpu.VMEM((tok, width), BF16),
            pltpu.VMEM((tok, cols), BF16),
            pltpu.VMEM((tok, 2 * cols), BF16),
            pltpu.VMEM((tok, HEAD_DIM), F32),
            pltpu.SMEM((n,), jnp.int32),
            pltpu.SMEM((n,), jnp.int32),
            pltpu.SMEM((n,), jnp.int32),
            pltpu.VMEM((tok, cols), BF16),
            pltpu.VMEM((tok, cols), BF16),
            pltpu.VMEM(prompt_keys.shape, BF16),
            pltpu.VMEM(prompt_keys.shape, BF16),
            pltpu.VMEM((2, roots // 2, 2, tok, cols), BF16),
            pltpu.VMEM((n, 2, slab_rows, cols), BF16),
            pltpu.VMEM((heads, tok, 2 * HEAD_DIM), F32),
            pltpu.VMEM((heads, tok, HEAD_DIM), F32),
            pltpu.VMEM((2, half, cols), BF16),
            pltpu.VMEM((roots // 2, 2, tok, cols), BF16),
            pltpu.VMEM((roots // 2, tok, cols), BF16),
            pltpu.VMEM((roots // 2, tok, cols), BF16),
            pltpu.VMEM((chunks, Z - 1, roots // 2, rz, cols), BF16),
            pltpu.VMEM((2, padded, cols), BF16),
            pltpu.VMEM((2, padded, cols), BF16),
            pltpu.SemaphoreType.DMA((n_copies,)),
            pltpu.SemaphoreType.DMA((n_copies,)),
            pltpu.SemaphoreType.DMA((8,)),
            pltpu.SemaphoreType.DMA((groups,)),
        ],
        compiler_params=pltpu.CompilerParams(
            collective_id=0, has_side_effects=True, vmem_limit_bytes=63 * 2**20
        ),
    )(
        parent, fork_tokens, lengths, queries, branch_keys, branch_values, prompt_keys,
        prompt_values,
    )

def solution(mesh):
    placed = (
        P("branch", "head"),
        P("branch", "head"),
        P("branch", "head"),
        P(("branch", "head"), None),
        P(("branch", "head"), None),
        P(),
        P(),
        P(),
    )
    return jax.shard_map(
        functools.partial(body, mesh.shape["branch"], mesh.shape["head"]),
        mesh=mesh, in_specs=placed, out_specs=P("branch", "head"), check_vma=False,
    )
```

```python
import functools
import math

import jax
import jax.numpy as jnp
from jax import lax
from jax.experimental import pallas as pl
from jax.experimental.pallas import tpu as pltpu
from jax.sharding import PartitionSpec as P

HEADS = 64
KV_HEADS = 8
HEAD_DIM = 128
MESH = pl.DeviceIdType.MESH
F32 = jnp.float32
BF16 = jnp.bfloat16


def place(n):
    me = lax.axis_index("branch")
    return me, me // 4, (me // 2) % 2, me % 2, lax.axis_index("head")


def root_rank(parent_ref, index, n):
    before = jnp.int32(0)
    for j in range(n):
        before = before + jnp.where((parent_ref[j] < 0) & (j < index), 1, 0)
    return before


def tree_kernel(
    n, heads_n, roots, chunks,
    parent_hbm, fork_hbm, length_hbm, q_hbm, bk_hbm, bv_hbm, pk_hbm, pv_hbm,
    out_hbm,
    q_ref, out_ref, keys_out, values_out, live_out, parent_ref, fork_ref, length_ref, bk_ref, bv_ref, pk_ref, pv_ref, roots_all,
    prompt_out, acc, tops, sib_kv, cand, x_in, part, z_in, y_out, y_in,
    send_sem, recv_sem, local_sem, out_sem,
):
    Z = n // 4
    tok, cols = bk_ref.shape
    half = tok // 2
    crows = tok // chunks
    rz = crows // Z
    groups = cols // HEAD_DIM
    per_group = q_ref.shape[1] // cols
    run = per_group // 2
    blocks = 2 * groups
    scale = math.log2(math.e) / math.sqrt(HEAD_DIM)
    contract = (((1,), (1,)), ((), ()))
    me, z, x, c, h = place(n)
    sib = me + 1 - 2 * c
    xp = me + 2 - 4 * x

    def zpeer(d):
        return lax.rem(z + d, Z) * 4 + x * 2 + c

    def zfrom(d):
        return lax.rem(z + Z - d, Z)

    local = []
    for i, (src, dst) in enumerate((
        (pk_hbm, pk_ref), (pv_hbm, pv_ref), (bk_hbm, bk_ref), (bv_hbm, bv_ref),
        (parent_hbm, parent_ref), (fork_hbm, fork_ref), (length_hbm, length_ref), (q_hbm, q_ref),
    )):
        cp = pltpu.make_async_copy(src, dst, local_sem.at[i])
        cp.start()
        local.append(cp)

    counter = [0]
    copies = []

    def copy(src, dst, b, hh=None):
        k = counter[0]
        counter[0] += 1
        cp = pltpu.make_async_remote_copy(
            src_ref=src, dst_ref=dst, send_sem=send_sem.at[k], recv_sem=recv_sem.at[k],
            device_id=(b, h if hh is None else hh), device_id_type=MESH,
        )
        cp.start()
        copies.append(cp)
        return cp

    def own_part(block):
        g = block // 2
        lanes = pl.ds(pl.multiple_of(g * HEAD_DIM, HEAD_DIM), HEAD_DIM)
        row = lax.broadcasted_iota(jnp.int32, (tok, tok), 0)
        causal = lax.broadcasted_iota(jnp.int32, (tok, tok), 1) <= row
        k = bk_ref[:, lanes]
        v = jnp.concatenate([bv_ref[:, lanes], jnp.ones((tok, HEAD_DIM), BF16)], 1)
        for i in range(run):
            head = block * run + i
            q = q_ref[:, pl.ds(pl.multiple_of(head * HEAD_DIM, HEAD_DIM), HEAD_DIM)]
            s = lax.dot_general(q, k, contract, preferred_element_type=F32)
            s = jnp.where(causal, s, -1e30)
            top = jnp.max(s, axis=1, keepdims=True)
            p = jnp.exp2((s - top) * scale).astype(BF16)
            acc[head] = jnp.dot(p, v, preferred_element_type=F32)
            tops[head] = jnp.broadcast_to(top, (tok, HEAD_DIM))

    def prompt_part(block):
        g = block // 2
        lanes = slice(g * HEAD_DIM, (g + 1) * HEAD_DIM)
        k = prompt_out[:, 0, :, lanes].reshape(-1, HEAD_DIM)
        v = prompt_out[:, 1, :, lanes].reshape(-1, HEAD_DIM)
        v = jnp.concatenate([v, jnp.ones(v.shape, BF16)], 1)
        for i in range(run):
            head = block * run + i
            q = q_ref[:, head * HEAD_DIM : (head + 1) * HEAD_DIM]
            total, top = absorb(head, q, k, v)
            acc[head] = total
            tops[head] = top

    def absorb(head, q, k, v):
        s = lax.dot_general(q, k, contract, preferred_element_type=F32)
        before = tops[head]
        top = jnp.maximum(before, jnp.max(s, axis=1, keepdims=True))
        p = jnp.exp2((s - top[:, :1]) * scale).astype(BF16)
        fade = jnp.exp2((before - top) * scale)
        fade = jnp.concatenate([fade, fade], 1)
        return jnp.dot(p, v, preferred_element_type=F32) + acc[head] * fade, top

    wide = per_group * HEAD_DIM

    def out_copy(g):
        span = pl.ds(pl.multiple_of(g * wide, wide), wide)
        return pltpu.make_async_copy(out_ref.at[:, span], out_hbm.at[:, span], out_sem.at[g])

    def parent_part(g, carry):
        k = keys_out[:, pl.ds(pl.multiple_of(g * HEAD_DIM, HEAD_DIM), HEAD_DIM)]
        v = values_out[:, pl.ds(pl.multiple_of(g * 2 * HEAD_DIM, 2 * HEAD_DIM), 2 * HEAD_DIM)]
        live = live_out[...] > 0.5
        for i in range(per_group):
            head = g * per_group + i
            here = pl.ds(pl.multiple_of(head * HEAD_DIM, HEAD_DIM), HEAD_DIM)
            total, _ = absorb(head, q_ref[:, here], k, v)
            result = total[:, :HEAD_DIM] / total[:, HEAD_DIM:]
            out_ref[:, here] = jnp.where(live, result, 0.0).astype(BF16)
        out_copy(g).start()
        return carry

    barrier = pltpu.get_barrier_semaphore()
    peers = [(sib, h), (xp, h)] + [(zpeer(d), h) for d in range(1, Z)]
    if heads_n == 2:
        peers.append((me, 1 - h))
    for peer in peers:
        pl.semaphore_signal(barrier, inc=1, device_id=peer, device_id_type=MESH)
    pl.semaphore_wait(barrier, len(peers))

    theirs = pl.ds(pl.multiple_of((1 - c) * half, half), half)
    mine = pl.ds(pl.multiple_of(c * half, half), half)
    cp_kv = [copy(bk_hbm.at[theirs], sib_kv.at[0], sib), copy(bv_hbm.at[theirs], sib_kv.at[1], sib)]

    local[0].wait()
    local[1].wait()
    if heads_n == 2:
        rows = pk_ref.shape[0]
        away = pl.ds(pl.multiple_of((1 - h) * cols, cols), cols)
        home = pl.ds(pl.multiple_of(h * cols, cols), cols)
        pad = jnp.zeros((y_out.shape[1] - rows, cols), F32)
        for i, ref in enumerate((pk_ref, pv_ref)):
            y_out[i] = jnp.concatenate([ref[:, away].astype(F32), pad], 0).astype(BF16)
        cp_y = copy(y_out, y_in, me, 1 - h)

    if heads_n == 2:
        cp_y.wait_recv()
        for i, ref in enumerate((pk_ref, pv_ref)):
            prompt_out[me, i] = jnp.concatenate(
                [ref[:, home].astype(F32), y_in[i, :rows].astype(F32)], 0
            ).astype(BF16)
    else:
        prompt_out[me, 0] = pk_ref[...]
        prompt_out[me, 1] = pv_ref[...]
    cp_pz, cp_px, cp_ps = {}, {}, []
    for i in range(2):
        slab = prompt_out.at[me, i]
        for d in range(1, Z):
            cp_pz[i, d] = copy(slab, slab, zpeer(d))
    for i in range(2):
        slab = prompt_out.at[me, i]
        cp_px[i, 0] = copy(slab, slab, xp)
        cp_ps.append(copy(slab, slab, sib))

    def prompt_step(i):
        for d in range(1, Z):
            cp_pz[i, d].wait_recv()
            got = prompt_out.at[zfrom(d) * 4 + x * 2 + c, i]
            cp_px[i, d] = copy(got, got, xp)
            cp_ps.append(copy(got, got, sib))

    def prompt_last(i):
        for d in range(0, Z):
            cp_px[i, d].wait_recv()
            got = prompt_out.at[zfrom(d) * 4 + (1 - x) * 2 + c, i]
            cp_ps.append(copy(got, got, sib))

    for cp in local[2:]:
        cp.wait()
    is_me, rank_me = parent_ref[me] < 0, root_rank(parent_ref, me, n)
    is_sib, rank_sib = parent_ref[sib] < 0, root_rank(parent_ref, sib, n)

    cp_x = []
    for i, ref in enumerate((bk_ref, bv_ref)):
        cp_kv[i].wait_recv()
        for r in range(roots):
            w_me = jnp.where(is_me & (rank_me == r), 1.0, 0.0).astype(F32)
            w_sib = jnp.where(is_sib & (rank_sib == r), 1.0, 0.0).astype(F32)
            total = ref[mine, :].astype(F32) * w_me + sib_kv[i].astype(F32) * w_sib
            cand[r // 2, r % 2, i * half : (i + 1) * half] = total.astype(BF16)
        if chunks == 2 or i == 1:
            span = slice((i + 1) * half - crows, (i + 1) * half)
            cp_x.append(copy(cand.at[:, 1 - x, span], x_in.at[:, span], xp))

    def own_loop(block, carry):
        own_part(block)
        return carry

    lax.fori_loop(0, blocks // 2, own_loop, 0)
    prompt_step(0)
    lax.fori_loop(blocks // 2, blocks, own_loop, 0)
    prompt_step(1)

    def zrows(ch, zz):
        return pl.ds(pl.multiple_of(ch * crows + zz * rz, rz), rz)

    cp_rs = {}
    for ch in range(chunks):
        cp_x[ch].wait_recv()
        span = slice(ch * crows, (ch + 1) * crows)
        for j in range(roots // 2):
            part[j, span] = (cand[j, x, span].astype(F32) + x_in[j, span].astype(F32)).astype(BF16)
        for d in range(1, Z):
            cp_rs[ch, d] = copy(
                part.at[:, zrows(ch, lax.rem(z + d, Z))], z_in.at[ch, d - 1], zpeer(d)
            )

    def piece(ch, xx, zz):
        return roots_all.at[c, :, xx, zrows(ch, zz)]

    cp_gz, cp_gx, cp_gs = {}, {}, []

    def reduce_step(ch):
        for d in range(1, Z):
            cp_rs[ch, d].wait_recv()
        for j in range(roots // 2):
            total = part[j, zrows(ch, z)].astype(F32)
            for d in range(1, Z):
                total = total + z_in[ch, d - 1, j].astype(F32)
            roots_all[c, j, x, zrows(ch, z)] = total.astype(BF16)
        own = piece(ch, x, z)
        for d in range(1, Z):
            cp_gz[ch, d] = copy(own, own, zpeer(d))
        cp_gx[ch, 0] = copy(own, own, xp)
        cp_gs.append(copy(own, own, sib))

    def gather_step(ch):
        for d in range(1, Z):
            cp_gz[ch, d].wait_recv()
            got = piece(ch, x, zfrom(d))
            cp_gx[ch, d] = copy(got, got, xp)
            cp_gs.append(copy(got, got, sib))

    def last_step(ch):
        for d in range(0, Z):
            cp_gx[ch, d].wait_recv()
            got = piece(ch, 1 - x, zfrom(d))
            cp_gs.append(copy(got, got, sib))

    for i in range(2):
        prompt_last(i)
    for cp in cp_ps:
        cp.wait_recv()

    at = {}
    for step, ch, when in (
        (reduce_step, 0, 1), (reduce_step, 1, 2), (gather_step, 0, 4), (gather_step, 1, 5),
        (last_step, 0, 6), (last_step, 1, 7),
    ):
        if ch < chunks:
            at.setdefault(max(when * blocks // 8 - 1, 0), []).append((step, ch))
    for block in range(blocks):
        prompt_part(block)
        for step, ch in at.get(block, []):
            step(ch)

    rank = root_rank(parent_ref, jnp.maximum(parent_ref[me], 0), n)
    fork = fork_ref[me]
    weights = [jnp.where(rank == r, 1.0, 0.0).astype(F32) for r in range(roots)]
    live_out[...] = jnp.where(
        lax.broadcasted_iota(jnp.int32, (tok, HEAD_DIM), 0) < length_ref[me], 1.0, 0.0
    )
    for cp in cp_gs:
        cp.wait_recv()
    first = bk_ref[0:1, :].astype(F32)
    for i in range(2):
        out_rows = slice(i * half, (i + 1) * half)
        seen = i * half + lax.broadcasted_iota(jnp.int32, (half, cols), 0) < fork
        sums = []
        for start in (0, half):
            total = jnp.zeros((half, cols), F32)
            for r in range(roots):
                total = total + weights[r] * roots_all[
                    i, r // 2, r % 2, start : start + half
                ].astype(F32)
            sums.append(total)
        keys_out[out_rows] = jnp.where(seen, sums[0], first).astype(BF16)
        values = jnp.where(seen, sums[1], 0.0).astype(BF16)
        ones = jnp.where(seen[:, :HEAD_DIM], 1.0, 0.0).astype(BF16)
        for g in range(groups):
            values_out[out_rows, 2 * g * HEAD_DIM : (2 * g + 1) * HEAD_DIM] = values[
                :, g * HEAD_DIM : (g + 1) * HEAD_DIM
            ]
            values_out[out_rows, (2 * g + 1) * HEAD_DIM : (2 * g + 2) * HEAD_DIM] = ones
    lax.fori_loop(0, groups, parent_part, 0)
    for cp in copies:
        cp.wait_send()
    for g in range(groups):
        out_copy(g).wait()


def body(
    n, heads_n, queries, branch_keys, branch_values, prompt_keys, prompt_values, parent,
    fork_tokens, lengths,
):
    tok, cols = branch_keys.shape
    groups = cols // HEAD_DIM
    per_group = HEADS // KV_HEADS
    roots = n // 8
    Z = n // 4
    half = tok // 2
    rows = prompt_keys.shape[0]
    slab_rows = rows * heads_n
    if heads_n != 2:
        prompt_keys = lax.all_to_all(prompt_keys, "head", split_axis=1, concat_axis=0, tiled=True)
        prompt_values = lax.all_to_all(
            prompt_values, "head", split_axis=1, concat_axis=0, tiled=True
        )
    padded = -(-rows // 16) * 16
    hbm = pl.BlockSpec(memory_space=pltpu.HBM)
    chunks = 2 if half % (16 * Z) == 0 else 1
    rz = tok // chunks // Z
    n_copies = 16 + 20 * Z
    width = queries.shape[1]
    heads = width // HEAD_DIM
    return pl.pallas_call(
        functools.partial(tree_kernel, n, heads_n, roots, chunks),
        out_shape=jax.ShapeDtypeStruct((tok, width), BF16),
        in_specs=[hbm] * 8,
        out_specs=hbm,
        scratch_shapes=[
            pltpu.VMEM((tok, width), BF16),
            pltpu.VMEM((tok, width), BF16),
            pltpu.VMEM((tok, cols), BF16),
            pltpu.VMEM((tok, 2 * cols), BF16),
            pltpu.VMEM((tok, HEAD_DIM), F32),
            pltpu.SMEM((n,), jnp.int32),
            pltpu.SMEM((n,), jnp.int32),
            pltpu.SMEM((n,), jnp.int32),
            pltpu.VMEM((tok, cols), BF16),
            pltpu.VMEM((tok, cols), BF16),
            pltpu.VMEM(prompt_keys.shape, BF16),
            pltpu.VMEM(prompt_keys.shape, BF16),
            pltpu.VMEM((2, roots // 2, 2, tok, cols), BF16),
            pltpu.VMEM((n, 2, slab_rows, cols), BF16),
            pltpu.VMEM((heads, tok, 2 * HEAD_DIM), F32),
            pltpu.VMEM((heads, tok, HEAD_DIM), F32),
            pltpu.VMEM((2, half, cols), BF16),
            pltpu.VMEM((roots // 2, 2, tok, cols), BF16),
            pltpu.VMEM((roots // 2, tok, cols), BF16),
            pltpu.VMEM((roots // 2, tok, cols), BF16),
            pltpu.VMEM((chunks, Z - 1, roots // 2, rz, cols), BF16),
            pltpu.VMEM((2, padded, cols), BF16),
            pltpu.VMEM((2, padded, cols), BF16),
            pltpu.SemaphoreType.DMA((n_copies,)),
            pltpu.SemaphoreType.DMA((n_copies,)),
            pltpu.SemaphoreType.DMA((8,)),
            pltpu.SemaphoreType.DMA((groups,)),
        ],
        compiler_params=pltpu.CompilerParams(
            collective_id=0, has_side_effects=True, vmem_limit_bytes=63 * 2**20
        ),
    )(
        parent, fork_tokens, lengths, queries, branch_keys, branch_values, prompt_keys,
        prompt_values,
    )

def solution(mesh):
    placed = (
        P("branch", "head"),
        P("branch", "head"),
        P("branch", "head"),
        P(("branch", "head"), None),
        P(("branch", "head"), None),
        P(),
        P(),
        P(),
    )
    return jax.shard_map(
        functools.partial(body, mesh.shape["branch"], mesh.shape["head"]),
        mesh=mesh, in_specs=placed, out_specs=P("branch", "head"), check_vma=False,
    )
```

```python
import functools
import math

import jax
import jax.numpy as jnp
from jax import lax
from jax.experimental import pallas as pl
from jax.experimental.pallas import tpu as pltpu
from jax.sharding import PartitionSpec as P

HEADS = 64
KV_HEADS = 8
HEAD_DIM = 128
MESH = pl.DeviceIdType.MESH
F32 = jnp.float32
BF16 = jnp.bfloat16


def place(n):
    me = lax.axis_index("branch")
    return me, me // 4, (me // 2) % 2, me % 2, lax.axis_index("head")


def root_rank(parent_ref, index, n):
    before = jnp.int32(0)
    for j in range(n):
        before = before + jnp.where((parent_ref[j] < 0) & (j < index), 1, 0)
    return before


def tree_kernel(
    n, heads_n, roots, chunks,
    parent_hbm, fork_hbm, length_hbm, q_hbm, bk_hbm, bv_hbm, pk_hbm, pv_hbm,
    out_hbm,
    q_ref, out_ref, keys_out, values_out, live_out, parent_ref, fork_ref, length_ref, bk_ref, bv_ref, pk_ref, pv_ref, roots_all,
    prompt_out, acc, tops, acc_next, tops_next, sib_kv, cand, x_in, part, z_in, y_out, y_in,
    send_sem, recv_sem, local_sem, out_sem,
):
    Z = n // 4
    tok, cols = bk_ref.shape
    half = tok // 2
    crows = tok // chunks
    rz = crows // Z
    groups = cols // HEAD_DIM
    per_group = q_ref.shape[1] // cols
    run = per_group // 2
    blocks = 2 * groups
    scale = math.log2(math.e) / math.sqrt(HEAD_DIM)
    contract = (((1,), (1,)), ((), ()))
    me, z, x, c, h = place(n)
    sib = me + 1 - 2 * c
    xp = me + 2 - 4 * x

    def zpeer(d):
        return lax.rem(z + d, Z) * 4 + x * 2 + c

    def zfrom(d):
        return lax.rem(z + Z - d, Z)

    local = []
    for i, (src, dst) in enumerate((
        (pk_hbm, pk_ref), (pv_hbm, pv_ref), (bk_hbm, bk_ref), (bv_hbm, bv_ref),
        (parent_hbm, parent_ref), (fork_hbm, fork_ref), (length_hbm, length_ref), (q_hbm, q_ref),
    )):
        cp = pltpu.make_async_copy(src, dst, local_sem.at[i])
        cp.start()
        local.append(cp)

    counter = [0]
    copies = []

    def make(src, dst, b, hh=None, when=None, lands=None):
        k = counter[0]
        counter[0] += 1
        cp = pltpu.make_async_remote_copy(
            src_ref=src, dst_ref=dst, send_sem=send_sem.at[k],
            recv_sem=recv_sem.at[k if lands is None else lands],
            device_id=(b, h if hh is None else hh), device_id_type=MESH,
        )
        copies.append((cp, when))
        return cp

    def copy(*args):
        cp = make(*args)
        cp.start()
        return cp

    def go(cp):
        when = next(w for other, w in copies if other is cp)
        if when is None:
            cp.start()
        else:
            pl.when(when)(cp.start)

    line = Z == 4

    def z_plan(view):
        sends, numbers, passes = {}, {}, []
        for d in range(1, Z):
            numbers[d] = counter[0]
            skip = None
            if line and d != 2:
                skip = z != (3 if d == 1 else 0)
            sends[d] = make(view(z), view(z), zpeer(d), None, skip)
        if line:
            for at_z, item, to, d in ((1, 3, 0, 1), (2, 0, 3, 3)):
                passes.append(make(
                    view(item), view(item), to * 4 + x * 2 + c, None, z == at_z, numbers[d]
                ))
        return sends, passes

    def z_start(plan):
        for cp in plan[0].values():
            go(cp)

    def z_finish(plan):
        plan[0][2].wait_recv()
        for cp in plan[1]:
            go(cp)
        for d, cp in plan[0].items():
            if d != 2:
                cp.wait_recv()

    class Spread:
        def __init__(self, view):
            self.z = z_plan(functools.partial(view, x))
            self.x = [make(view(x, zfrom(d)), view(x, zfrom(d)), xp) for d in range(Z)]
            self.core = [
                make(view(xx, zfrom(d)), view(xx, zfrom(d)), sib)
                for xx in (x, 1 - x) for d in range(Z)
            ]

        def begin(self):
            z_start(self.z)
            go(self.x[0])
            go(self.core[0])

        def middle(self):
            z_finish(self.z)
            for d in range(1, Z):
                go(self.x[d])
                go(self.core[d])

        def last(self):
            for d in range(Z):
                self.x[d].wait_recv()
                go(self.core[Z + d])

        def done(self):
            for cp in self.core:
                cp.wait_recv()

    def own_part(block):
        g = block // 2
        lanes = pl.ds(pl.multiple_of(g * HEAD_DIM, HEAD_DIM), HEAD_DIM)
        row = lax.broadcasted_iota(jnp.int32, (tok, tok), 0)
        causal = lax.broadcasted_iota(jnp.int32, (tok, tok), 1) <= row
        k = bk_ref[:, lanes]
        v = jnp.concatenate([bv_ref[:, lanes], jnp.ones((tok, HEAD_DIM), BF16)], 1)
        for i in range(run):
            head = block * run + i
            q = q_ref[:, pl.ds(pl.multiple_of(head * HEAD_DIM, HEAD_DIM), HEAD_DIM)]
            s = lax.dot_general(q, k, contract, preferred_element_type=F32)
            s = jnp.where(causal, s, -1e30)
            top = jnp.max(s, axis=1, keepdims=True)
            p = jnp.exp2((s - top) * scale).astype(BF16)
            acc[head] = jnp.dot(p, v, preferred_element_type=F32)
            tops[head] = jnp.broadcast_to(top, (tok, HEAD_DIM))

    def prompt_part(block):
        g = block // 2
        lanes = pl.ds(pl.multiple_of(g * HEAD_DIM, HEAD_DIM), HEAD_DIM)
        k = prompt_out[:, 0, :, lanes].reshape(-1, HEAD_DIM)
        v = prompt_out[:, 1, :, lanes].reshape(-1, HEAD_DIM)
        v = jnp.concatenate([v, jnp.ones(v.shape, BF16)], 1)
        for i in range(run):
            head = block * run + i
            q = q_ref[:, pl.ds(pl.multiple_of(head * HEAD_DIM, HEAD_DIM), HEAD_DIM)]
            acc_next[head], tops_next[head] = absorb(acc[head], tops[head], q, k, v)

    def absorb(total, before, q, k, v):
        s = lax.dot_general(q, k, contract, preferred_element_type=F32)
        top = jnp.maximum(before, jnp.max(s, axis=1, keepdims=True))
        p = jnp.exp2((s - top[:, :1]) * scale).astype(BF16)
        fade = jnp.exp2((before - top) * scale)
        fade = jnp.concatenate([fade, fade], 1)
        return jnp.dot(p, v, preferred_element_type=F32) + total * fade, top

    wide = per_group * HEAD_DIM

    def out_copy(g):
        span = pl.ds(pl.multiple_of(g * wide, wide), wide)
        return pltpu.make_async_copy(out_ref.at[:, span], out_hbm.at[:, span], out_sem.at[g])

    def parent_part(g, carry):
        k = keys_out[:, pl.ds(pl.multiple_of(g * HEAD_DIM, HEAD_DIM), HEAD_DIM)]
        v = values_out[:, pl.ds(pl.multiple_of(g * 2 * HEAD_DIM, 2 * HEAD_DIM), 2 * HEAD_DIM)]
        live = live_out[...] > 0.5
        for i in range(per_group):
            head = g * per_group + i
            here = pl.ds(pl.multiple_of(head * HEAD_DIM, HEAD_DIM), HEAD_DIM)
            total, _ = absorb(acc_next[head], tops_next[head], q_ref[:, here], k, v)
            result = total[:, :HEAD_DIM] / total[:, HEAD_DIM:]
            out_ref[:, here] = jnp.where(live, result, 0.0).astype(BF16)
        out_copy(g).start()
        return carry

    barrier = pltpu.get_barrier_semaphore()
    peers = [(sib, h), (xp, h)] + [(zpeer(d), h) for d in range(1, Z)]
    if heads_n == 2:
        peers.append((me, 1 - h))
    for peer in peers:
        pl.semaphore_signal(barrier, inc=1, device_id=peer, device_id_type=MESH)
    pl.semaphore_wait(barrier, len(peers))

    theirs = pl.ds(pl.multiple_of((1 - c) * half, half), half)
    mine = pl.ds(pl.multiple_of(c * half, half), half)
    cp_kv = [copy(bk_hbm.at[theirs], sib_kv.at[0], sib), copy(bv_hbm.at[theirs], sib_kv.at[1], sib)]

    local[0].wait()
    local[1].wait()
    if heads_n == 2:
        rows = pk_ref.shape[0]
        away = pl.ds(pl.multiple_of((1 - h) * cols, cols), cols)
        home = pl.ds(pl.multiple_of(h * cols, cols), cols)
        pad = jnp.zeros((y_out.shape[1] - rows, cols), F32)
        for i, ref in enumerate((pk_ref, pv_ref)):
            y_out[i] = jnp.concatenate([ref[:, away].astype(F32), pad], 0).astype(BF16)
        cp_y = copy(y_out, y_in, me, 1 - h)

    if heads_n == 2:
        cp_y.wait_recv()
        for i, ref in enumerate((pk_ref, pv_ref)):
            prompt_out[me, i] = jnp.concatenate(
                [ref[:, home].astype(F32), y_in[i, :rows].astype(F32)], 0
            ).astype(BF16)
    else:
        prompt_out[me, 0] = pk_ref[...]
        prompt_out[me, 1] = pv_ref[...]
    def prompt_view(i, xx, zz):
        return prompt_out.at[zz * 4 + xx * 2 + c, i]

    prompt_ways = [Spread(functools.partial(prompt_view, i)) for i in range(2)]
    for way in prompt_ways:
        way.begin()

    for cp in local[2:]:
        cp.wait()
    is_me, rank_me = parent_ref[me] < 0, root_rank(parent_ref, me, n)
    is_sib, rank_sib = parent_ref[sib] < 0, root_rank(parent_ref, sib, n)

    cp_x = []
    for i, ref in enumerate((bk_ref, bv_ref)):
        cp_kv[i].wait_recv()
        for r in range(roots):
            w_me = jnp.where(is_me & (rank_me == r), 1.0, 0.0).astype(F32)
            w_sib = jnp.where(is_sib & (rank_sib == r), 1.0, 0.0).astype(F32)
            total = ref[mine, :].astype(F32) * w_me + sib_kv[i].astype(F32) * w_sib
            cand[r // 2, r % 2, i * half : (i + 1) * half] = total.astype(BF16)
        if chunks == 2 or i == 1:
            span = slice((i + 1) * half - crows, (i + 1) * half)
            cp_x.append(copy(cand.at[:, 1 - x, span], x_in.at[:, span], xp))

    def own_loop(block, carry):
        own_part(block)
        pl.when(block == blocks // 2 - 1)(prompt_ways[0].middle)
        return carry

    lax.fori_loop(0, blocks, own_loop, 0)
    prompt_ways[1].middle()

    def zrows(ch, zz):
        return pl.ds(pl.multiple_of(ch * crows + zz * rz, rz), rz)

    cp_rs = {}
    for ch in range(chunks):
        cp_x[ch].wait_recv()
        span = slice(ch * crows, (ch + 1) * crows)
        for j in range(roots // 2):
            part[j, span] = (cand[j, x, span].astype(F32) + x_in[j, span].astype(F32)).astype(BF16)
        for d in range(1, Z):
            cp_rs[ch, d] = copy(
                part.at[:, zrows(ch, lax.rem(z + d, Z))], z_in.at[ch, d - 1], zpeer(d)
            )

    def piece(ch, xx, zz):
        return roots_all.at[c, :, xx, zrows(ch, zz)]

    root_ways = [Spread(functools.partial(piece, ch)) for ch in range(chunks)]

    def reduce_step(ch):
        for d in range(1, Z):
            cp_rs[ch, d].wait_recv()
        for j in range(roots // 2):
            total = part[j, zrows(ch, z)].astype(F32)
            for d in range(1, Z):
                total = total + z_in[ch, d - 1, j].astype(F32)
            roots_all[c, j, x, zrows(ch, z)] = total.astype(BF16)
        root_ways[ch].begin()

    for way in prompt_ways:
        way.last()
    for way in prompt_ways:
        way.done()

    steps = {}
    for ch in range(chunks):
        for step, when in (
            (functools.partial(reduce_step, ch), 1 + ch),
            (root_ways[ch].middle, 4 + ch),
            (root_ways[ch].last, 6 + ch),
        ):
            steps.setdefault(max(when * blocks // 8 - 1, 0), []).append(step)

    def prompt_loop(block, carry):
        prompt_part(block)
        for when, todo in steps.items():
            def run_steps(todo=todo):
                for step in todo:
                    step()
            pl.when(block == when)(run_steps)
        return carry

    lax.fori_loop(0, blocks, prompt_loop, 0)

    rank = root_rank(parent_ref, jnp.maximum(parent_ref[me], 0), n)
    fork = fork_ref[me]
    weights = [jnp.where(rank == r, 1.0, 0.0).astype(F32) for r in range(roots)]
    live_out[...] = jnp.where(
        lax.broadcasted_iota(jnp.int32, (tok, HEAD_DIM), 0) < length_ref[me], 1.0, 0.0
    )
    for way in root_ways:
        way.done()
    first = bk_ref[0:1, :].astype(F32)
    for i in range(2):
        out_rows = slice(i * half, (i + 1) * half)
        seen = i * half + lax.broadcasted_iota(jnp.int32, (half, cols), 0) < fork
        sums = []
        for start in (0, half):
            total = jnp.zeros((half, cols), F32)
            for r in range(roots):
                total = total + weights[r] * roots_all[
                    i, r // 2, r % 2, start : start + half
                ].astype(F32)
            sums.append(total)
        keys_out[out_rows] = jnp.where(seen, sums[0], first).astype(BF16)
        values = jnp.where(seen, sums[1], 0.0).astype(BF16)
        ones = jnp.where(seen[:, :HEAD_DIM], 1.0, 0.0).astype(BF16)
        for g in range(groups):
            values_out[out_rows, 2 * g * HEAD_DIM : (2 * g + 1) * HEAD_DIM] = values[
                :, g * HEAD_DIM : (g + 1) * HEAD_DIM
            ]
            values_out[out_rows, (2 * g + 1) * HEAD_DIM : (2 * g + 2) * HEAD_DIM] = ones
    lax.fori_loop(0, groups, parent_part, 0)
    for cp, when in copies:
        if when is None:
            cp.wait_send()
        else:
            pl.when(when)(cp.wait_send)
    for g in range(groups):
        out_copy(g).wait()


def body(
    n, heads_n, queries, branch_keys, branch_values, prompt_keys, prompt_values, parent,
    fork_tokens, lengths,
):
    tok, cols = branch_keys.shape
    groups = cols // HEAD_DIM
    per_group = HEADS // KV_HEADS
    roots = n // 8
    Z = n // 4
    half = tok // 2
    rows = prompt_keys.shape[0]
    slab_rows = rows * heads_n
    if heads_n != 2:
        prompt_keys = lax.all_to_all(prompt_keys, "head", split_axis=1, concat_axis=0, tiled=True)
        prompt_values = lax.all_to_all(
            prompt_values, "head", split_axis=1, concat_axis=0, tiled=True
        )
    padded = -(-rows // 16) * 16
    hbm = pl.BlockSpec(memory_space=pltpu.HBM)
    chunks = 2 if half % (16 * Z) == 0 else 1
    rz = tok // chunks // Z
    n_copies = 16 + 20 * Z
    width = queries.shape[1]
    heads = width // HEAD_DIM
    return pl.pallas_call(
        functools.partial(tree_kernel, n, heads_n, roots, chunks),
        out_shape=jax.ShapeDtypeStruct((tok, width), BF16),
        in_specs=[hbm] * 8,
        out_specs=hbm,
        scratch_shapes=[
            pltpu.VMEM((tok, width), BF16),
            pltpu.VMEM((tok, width), BF16),
            pltpu.VMEM((tok, cols), BF16),
            pltpu.VMEM((tok, 2 * cols), BF16),
            pltpu.VMEM((tok, HEAD_DIM), F32),
            pltpu.SMEM((n,), jnp.int32),
            pltpu.SMEM((n,), jnp.int32),
            pltpu.SMEM((n,), jnp.int32),
            pltpu.VMEM((tok, cols), BF16),
            pltpu.VMEM((tok, cols), BF16),
            pltpu.VMEM(prompt_keys.shape, BF16),
            pltpu.VMEM(prompt_keys.shape, BF16),
            pltpu.VMEM((2, roots // 2, 2, tok, cols), BF16),
            pltpu.VMEM((n, 2, slab_rows, cols), BF16),
            pltpu.VMEM((heads, tok, 2 * HEAD_DIM), F32),
            pltpu.VMEM((heads, tok, HEAD_DIM), F32),
            pltpu.VMEM((heads, tok, 2 * HEAD_DIM), F32),
            pltpu.VMEM((heads, tok, HEAD_DIM), F32),
            pltpu.VMEM((2, half, cols), BF16),
            pltpu.VMEM((roots // 2, 2, tok, cols), BF16),
            pltpu.VMEM((roots // 2, tok, cols), BF16),
            pltpu.VMEM((roots // 2, tok, cols), BF16),
            pltpu.VMEM((chunks, Z - 1, roots // 2, rz, cols), BF16),
            pltpu.VMEM((2, padded, cols), BF16),
            pltpu.VMEM((2, padded, cols), BF16),
            pltpu.SemaphoreType.DMA((n_copies,)),
            pltpu.SemaphoreType.DMA((n_copies,)),
            pltpu.SemaphoreType.DMA((8,)),
            pltpu.SemaphoreType.DMA((groups,)),
        ],
        compiler_params=pltpu.CompilerParams(
            collective_id=0, has_side_effects=True, vmem_limit_bytes=63 * 2**20
        ),
    )(
        parent, fork_tokens, lengths, queries, branch_keys, branch_values, prompt_keys,
        prompt_values,
    )

def solution(mesh):
    placed = (
        P("branch", "head"),
        P("branch", "head"),
        P("branch", "head"),
        P(("branch", "head"), None),
        P(("branch", "head"), None),
        P(),
        P(),
        P(),
    )
    return jax.shard_map(
        functools.partial(body, mesh.shape["branch"], mesh.shape["head"]),
        mesh=mesh, in_specs=placed, out_specs=P("branch", "head"), check_vma=False,
    )
```
